512 devices in a mesh: slab: 8 (over y, core), tile: 64 (over z, x).
Axes of the slice: x: 4, y: 4, z: 16, core: 2. Of those that a mesh axis runs over, the one named last changes fastest.
Arguments:
- depth_layers: float32 [8, 64, 512, 512], P('slab', 'tile'), may hold values from 1 to 3
- thickness_layers: float32 [8, 64, 512, 512], P('slab', 'tile'), may hold values from 0.05 to 0.5
- coverage: int32 [64, 512, 512], P('tile', 'slab'), may hold values 0 or 1
Outputs:
- smooth_depth: float32 [64, 512, 512], P('tile', 'slab')
- shade: float32 [64, 512, 512], P('tile', 'slab')
The draws below stay inside these ranges and needn't reach their ends.
All inputs are finite; a program needn't handle non-finite values. No bound on the sum of `coverage` on one device may be relied on, other than what follows from the above.
Results may differ from the reference program's by a relative error of at most 0.00002.
Values sent between devices are 32-bit elements; how exact they have to be, the bound alone decides.
No kernel may reach another device: no remote copies, remote signals or barrier semaphores. Data moves between devices by JAX's collectives and lax.ppermute only.
A program may use at most 64 MiB of HBM per device.

```python
import math
import jax
import jax.numpy as jnp
from jax import lax

TH = 512
TW = 512
SWEEPS = 4
SLABS = 8
TILES = 64
GRID = 8


def touch_ends(result, rng, smallest, top_value):
    longest = result.shape.index(max(result.shape))
    spots = []
    for shift in (0, 1):
        where = [jax.random.randint(jax.random.fold_in(rng, axis), (), 0, length) for axis, length in enumerate(result.shape)]
        where[longest] = (where[longest] + shift) % result.shape[longest]
        spots.append(tuple(where))
    return result.at[spots[0]].set(smallest).at[spots[1]].set(top_value)


def levels(rng, dims, split, smallest, high):
    loudness, own = 1.0, jax.random.fold_in(rng, 6)
    for axis_at, parts in split:
        draws = jnp.exp(jax.random.uniform(jax.random.fold_in(own, axis_at), (parts,), jnp.float32, smallest / len(split), high / len(split)))
        loudness = loudness * jnp.repeat(draws, dims[axis_at] // parts).reshape([-1 if axis == axis_at else 1 for axis in range(len(dims))])
    return loudness


def setup_inputs(seed: int = 0) -> dict:
    streams_of = jax.random.split(jax.random.key(seed), 4)
    depth_layers = jnp.clip(1.0 + 2.0 * jax.random.uniform(streams_of[0], (SLABS, TILES, TH, TW), jnp.float32) ** levels(streams_of[0], (SLABS, TILES, TH, TW), ((0, 8), (1, 64)), -0.2, 0.2), 1.0, 3.0)
    thickness_layers = jnp.clip(jnp.exp(math.log(0.5) - 2.3025851 * jax.random.uniform(streams_of[1], (SLABS, TILES, TH, TW), jnp.float32) ** levels(streams_of[1], (SLABS, TILES, TH, TW), ((0, 8), (1, 64)), -0.2, 0.2)), 0.05, 0.5)
    coverage = touch_ends((jax.random.randint(streams_of[2], (TILES, TH, TW), 0, 4) < 3).astype(jnp.int32), jax.random.fold_in(streams_of[2], 1), 0, 1)
    return dict(depth_layers=depth_layers, thickness_layers=thickness_layers, coverage=coverage)


flow_step = 0.2

def assemble(tiles):
    return tiles.reshape(GRID, GRID, TH, TW).transpose(0, 2, 1, 3).reshape(GRID * TH, GRID * TW)

def disassemble(image):
    return image.reshape(GRID, TH, GRID, TW).transpose(0, 2, 1, 3).reshape(GRID * GRID, TH, TW)

def flow_sweep(extended):
    slope_x = (extended[1:-1, 2:] - extended[1:-1, :-2]) * 0.5
    slope_y = (extended[2:, 1:-1] - extended[:-2, 1:-1]) * 0.5
    norm_inv = lax.rsqrt(1.0 + slope_x * slope_x + slope_y * slope_y)
    normal_x = slope_x * norm_inv
    normal_y = slope_y * norm_inv
    divergence = (normal_x[1:-1, 2:] - normal_x[1:-1, :-2]) * 0.5 + (normal_y[2:, 1:-1] - normal_y[:-2, 1:-1]) * 0.5
    return extended[2:-2, 2:-2] + flow_step * divergence

def shading(extended, thickness, coverage):
    slope_x = (extended[1:-1, 2:] - extended[1:-1, :-2]) * 0.5
    slope_y = (extended[2:, 1:-1] - extended[:-2, 1:-1]) * 0.5
    norm_inv = lax.rsqrt(1.0 + slope_x * slope_x + slope_y * slope_y)
    diffuse = jnp.maximum((0.8 - 0.36 * slope_x - 0.48 * slope_y) * norm_inv, 0.0)
    gloss = jnp.maximum((0.9487 - 0.1897 * slope_x - 0.253 * slope_y) * norm_inv, 0.0) ** 16
    fluid = coverage.astype(jnp.float32)
    lit = 0.15 + 0.7 * jnp.exp(-0.8 * thickness) * diffuse + 0.4 * gloss
    return fluid * lit + (1.0 - fluid) * 0.05

def reference(depth_layers, thickness_layers, coverage):
    depth = lax.optimization_barrier(jnp.min(depth_layers, axis=0))
    thickness = lax.optimization_barrier(jnp.sum(thickness_layers, axis=0))
    surface = assemble(depth)
    for sweep_index in range(SWEEPS):
        surface = flow_sweep(jnp.pad(surface, 2, mode='edge'))
    shade = shading(jnp.pad(surface, 1, mode='edge'), assemble(thickness), assemble(coverage))
    return (disassemble(surface), disassemble(shade))
```

```python
import functools
import math

import jax
import jax.numpy as jnp
from jax import lax
from jax.experimental import pallas as pl
from jax.experimental.pallas import tpu as pltpu
from jax.sharding import PartitionSpec as P

SWEEPS = 4
FLOW_STEP = 0.2

PAD = 16
LANES = 128


def ring(value, step):
    count = lax.axis_size("slab")
    return lax.ppermute(value, "slab", [(i, (i + step) % count) for i in range(count)])


def reduce_bands(bands, combine, index):
    count = bands.shape[0]

    def share(offset):
        return lax.dynamic_index_in_dim(bands, (index + offset + count) % count, 0, keepdims=False)

    ahead = count // 2
    behind = count - 1 - ahead
    forward = share(ahead)
    backward = share(-behind)
    for distance in range(ahead, 0, -1):
        forward = ring(forward, 1)
        if distance > 1:
            forward = combine(forward, share(distance - 1))
        if distance <= behind:
            backward = ring(backward, -1)
            if distance > 1:
                backward = combine(backward, share(1 - distance))
    return share(0), forward, backward


def tile_edges(value, grid, slabs):
    tiles = grid * grid
    route = []
    for t in range(tiles - grid):
        upper = (slabs - 1) * tiles + t
        lower = t + grid
        route += [(upper, lower), (lower, upper)]
    return lax.ppermute(value, ("slab", "tile"), route)


def to_column(value, grid, step):
    route = []
    for t in range(grid * grid):
        if 0 <= t % grid + step < grid:
            route.append((t, t + step))
    return lax.ppermute(value, "tile", route)


def flow_kernel(
    rows,
    width,
    edge_ref,
    above_ref,
    band_ref,
    below_ref,
    left_ref,
    right_ref,
    thick_a_ref,
    thick_b_ref,
    thick_c_ref,
    cover_ref,
    smooth_ref,
    shade_ref,
    surface,
    partial,
    normal_y,
):
    blocks = width // LANES
    total = rows + 2 * PAD
    top = PAD
    bottom = PAD + rows
    lane = lax.broadcasted_iota(jnp.int32, (8, LANES), 1)

    for j in range(blocks):
        cols = pl.ds(j * LANES, LANES)
        surface[j, 0:PAD, :] = above_ref[:, cols]
        surface[j, top:bottom, :] = band_ref[:, cols]
        surface[j, bottom:total, :] = below_ref[:, cols]
    for r in range(0, total, 8):
        surface[blocks, r : r + 8, :] = jnp.where(
            lane < LANES // 2, right_ref[r : r + 8, :], left_ref[r : r + 8, :]
        )

    def refill():
        @pl.when(edge_ref[0] == 1)
        def _():
            for j in range(blocks + 1):
                surface[j, top - 2 : top, :] = jnp.broadcast_to(surface[j, top : top + 1, :], (2, LANES))

        @pl.when(edge_ref[1] == 1)
        def _():
            for j in range(blocks + 1):
                surface[j, bottom : bottom + 2, :] = jnp.broadcast_to(
                    surface[j, bottom - 1 : bottom, :], (2, LANES)
                )

        @pl.when(edge_ref[2] == 1)
        def _():
            for r in range(8, total - 8, 8):
                first = jnp.broadcast_to(surface[0, r : r + 8, 0:1], (8, LANES))
                surface[blocks, r : r + 8, :] = jnp.where(
                    lane >= LANES // 2, first, surface[blocks, r : r + 8, :]
                )

        @pl.when(edge_ref[3] == 1)
        def _():
            for r in range(8, total - 8, 8):
                last = jnp.broadcast_to(
                    surface[blocks - 1, r : r + 8, LANES - 1 : LANES], (8, LANES)
                )
                surface[blocks, r : r + 8, :] = jnp.where(
                    lane < LANES // 2, last, surface[blocks, r : r + 8, :]
                )

    def across(pieces):
        after = [pltpu.roll(p, LANES - 1, 1) for p in pieces]
        before = [pltpu.roll(p, 1, 1) for p in pieces]
        n = len(pieces)
        return [
            jnp.where(lane == LANES - 1, after[(j + 1) % n], after[j])
            - jnp.where(lane == 0, before[(j - 1) % n], before[j])
            for j in range(n)
        ]

    for _ in range(SWEEPS):
        refill()
        for r in range(8, total - 8, 8):
            here = [surface[j, r : r + 8, :] for j in range(blocks + 1)]
            wide_x = across(here)
            wide_y = [
                surface[j, r + 1 : r + 9, :] - surface[j, r - 1 : r + 7, :] for j in range(blocks + 1)
            ]
            inverse = [
                lax.rsqrt(1.0 + 0.25 * (x * x + y * y)) for x, y in zip(wide_x, wide_y)
            ]
            spread = across([x * w for x, w in zip(wide_x, inverse)])
            for j in range(blocks + 1):
                normal_y[j, r : r + 8, :] = wide_y[j] * inverse[j]
                partial[j, r : r + 8, :] = here[j] + (0.25 * FLOW_STEP) * spread[j]
        for r in range(8, total - 8, 8):
            for j in range(blocks + 1):
                surface[j, r : r + 8, :] = partial[j, r : r + 8, :] + (0.25 * FLOW_STEP) * (
                    normal_y[j, r + 1 : r + 9, :] - normal_y[j, r - 1 : r + 7, :]
                )

    refill()
    for r in range(0, rows, 8):
        here = [surface[j, top + r : top + r + 8, :] for j in range(blocks + 1)]
        wide_x = across(here)
        for j in range(blocks):
            cols = pl.ds(j * LANES, LANES)
            x = 0.5 * wide_x[j]
            y = 0.5 * (
                surface[j, top + r + 1 : top + r + 9, :] - surface[j, top + r - 1 : top + r + 7, :]
            )
            inverse = lax.rsqrt(1.0 + (x * x + y * y))
            diffuse = jnp.maximum((0.8 - 0.36 * x - 0.48 * y) * inverse, 0.0)
            gloss = jnp.maximum((0.9487 - 0.1897 * x - 0.253 * y) * inverse, 0.0)
            for _ in range(4):
                gloss = gloss * gloss
            thick = (
                thick_a_ref[r : r + 8, cols] + thick_b_ref[r : r + 8, cols] + thick_c_ref[r : r + 8, cols]
            )
            fluid = cover_ref[r : r + 8, cols].astype(jnp.float32)
            lit = 0.15 + 0.7 * jnp.exp(-0.8 * thick) * diffuse + 0.4 * gloss
            smooth_ref[r : r + 8, cols] = here[j]
            shade_ref[r : r + 8, cols] = fluid * lit + (1.0 - fluid) * 0.05


def local(depth_layers, thickness_layers, coverage):
    slabs = lax.axis_size("slab")
    grid = math.isqrt(lax.axis_size("tile"))
    slab = lax.axis_index("slab")
    tile = lax.axis_index("tile")
    _, _, height, width = depth_layers.shape
    rows = height // slabs
    first, last = slab == 0, slab == slabs - 1
    edges = jnp.stack(
        [
            first & (tile // grid == 0),
            last & (tile // grid == grid - 1),
            tile % grid == 0,
            tile % grid == grid - 1,
        ]
    ).astype(jnp.int32)

    parts = reduce_bands(depth_layers.reshape(slabs, rows, width), jnp.minimum, slab)
    band = jnp.minimum(jnp.minimum(parts[0], parts[1]), parts[2])

    head, tail = band[:PAD], band[-PAD:]
    above = ring(tail, 1)
    below = ring(head, -1)
    beyond = tile_edges(jnp.where(first, head, tail), grid, slabs)
    above = jnp.where(first, beyond, above)
    below = jnp.where(last, beyond, below)

    def column(start):
        cut = slice(start, start + LANES)
        return jnp.concatenate([above[:, cut], band[:, cut], below[:, cut]], axis=0)

    left = to_column(column(width - LANES), grid, 1)
    right = to_column(column(0), grid, -1)

    thickness_layers, band = lax.optimization_barrier((thickness_layers, band))
    thick = reduce_bands(thickness_layers.reshape(slabs, rows, width), jnp.add, slab)

    vmem = pl.BlockSpec(memory_space=pltpu.VMEM)
    total = rows + 2 * PAD
    blocks = width // LANES + 1
    out = jax.ShapeDtypeStruct((rows, width), jnp.float32)
    smooth, shade = pl.pallas_call(
        functools.partial(flow_kernel, rows, width),
        out_shape=(out, out),
        in_specs=[pl.BlockSpec(memory_space=pltpu.SMEM)] + [vmem] * 9,
        out_specs=(vmem, vmem),
        scratch_shapes=[pltpu.VMEM((blocks, total, LANES), jnp.float32)] * 3,
    )(edges, above, band, below, left, right, *thick, coverage[0])
    return (smooth[None], shade[None])


def solution(mesh):
    return jax.shard_map(
        local,
        mesh=mesh,
        in_specs=(
            P("slab", "tile", None, None),
            P("slab", "tile", None, None),
            P("tile", "slab", None),
        ),
        out_specs=(P("tile", "slab", None), P("tile", "slab", None)),
        check_vma=False,
    )
```

```python
import functools
import math

import jax
import jax.numpy as jnp
from jax import lax
from jax.experimental import pallas as pl
from jax.experimental.pallas import tpu as pltpu
from jax.sharding import PartitionSpec as P

SWEEPS = 4
FLOW_STEP = 0.2

PAD = 16
LANES = 128
PARAMS = pltpu.CompilerParams(vmem_limit_bytes=16 * 1024 * 1024)


def pick_kernel(flip, depth_ref, thick_ref, out_ref, sems):
    parity = (lax.axis_index("slab") + flip) % 2
    copies = [
        pltpu.make_async_copy(ref.at[:, parity], out_ref.at[k], sems.at[k])
        for k, ref in enumerate((depth_ref, thick_ref))
    ]
    for copy in copies:
        copy.start()
    for copy in copies:
        copy.wait()


def pair_cores(depth, thick):
    bands, rows, width = depth.shape
    shape = (bands // 2, 2, rows, width)

    layers = [
        pltpu.with_memory_space_constraint(a.reshape(shape), pltpu.HBM) for a in (depth, thick)
    ]

    def pick(flip):
        return pl.pallas_call(
            functools.partial(pick_kernel, flip),
            compiler_params=PARAMS,
            out_shape=pltpu.VMEM((2, bands // 2, rows, width), jnp.float32),
            in_specs=[pl.BlockSpec(memory_space=pltpu.HBM)] * 2,
            out_specs=pl.BlockSpec(memory_space=pltpu.VMEM),
            scratch_shapes=[pltpu.SemaphoreType.DMA((2,))],
        )(*layers)

    own = pick(0)
    got = lax.ppermute(pick(1), "slab", [(i, i ^ 1) for i in range(bands)])
    return jnp.minimum(own[0], got[0]), own[1] + got[1]


def to_owners(value):
    slabs = lax.axis_size("slab")
    groups = [list(range(parity, slabs, 2)) for parity in range(2)]
    return lax.all_to_all(
        value, "slab", split_axis=0, concat_axis=0, axis_index_groups=groups, tiled=True
    )


def to_owners_by_swaps(value, slab):
    slabs = lax.axis_size("slab")
    chips = slabs // 2
    chip = slab // 2

    def share(index):
        return lax.dynamic_index_in_dim(value, index, 0, keepdims=False)

    total = share(chip)
    for step in range(1, chips):
        route = [(i, (i // 2 ^ step) * 2 + i % 2) for i in range(slabs)]
        total = total + lax.ppermute(share(chip ^ step), "slab", route)
    return total


def neighbour_rows(band, grid, slabs, core):
    tiles = grid * grid
    across = []
    for t in range(tiles):
        for s in range(1, slabs, 2):
            upper = s * tiles + t
            lower = (s + 1) * tiles + t if s + 1 < slabs else t + grid
            if s + 1 < slabs or t + grid < tiles:
                across += [(upper, lower), (lower, upper)]
    odd = core == 1
    head, tail = band[:PAD], band[-PAD:]
    far = lax.ppermute(jnp.where(odd, tail, head), ("slab", "tile"), across)
    near = lax.ppermute(jnp.where(odd, head, tail), "slab", [(i, i ^ 1) for i in range(slabs)])
    return far, near


def neighbour_columns(first, last, grid, column):
    odd = column % 2 == 1
    near, far = [], []
    for t in range(grid * grid):
        if t % grid + 1 < grid:
            (near if t % 2 == 0 else far).extend([(t, t + 1), (t + 1, t)])
    far = lax.ppermute(jnp.where(odd, last, first), "tile", far)
    near = lax.ppermute(jnp.where(odd, first, last), "tile", near)
    return jnp.where(odd, near, far), jnp.where(odd, far, near)


def flow_kernel(
    rows,
    width,
    grid,
    slabs,
    above_ref,
    band_ref,
    below_ref,
    left_ref,
    right_ref,
    parts_ref,
    cover_ref,
    smooth_ref,
    shade_ref,
    surface,
    partial,
    normal_y,
):
    blocks = width // LANES
    total = rows + 2 * PAD
    top = PAD
    bottom = PAD + rows
    slab, tile = lax.axis_index("slab"), lax.axis_index("tile")
    top_edge = (slab == 0) & (tile < grid)
    bottom_edge = (slab == slabs - 1) & (tile >= grid * (grid - 1))
    left_edge = lax.rem(tile, grid) == 0
    right_edge = lax.rem(tile, grid) == grid - 1
    lane = lax.broadcasted_iota(jnp.int32, (8, LANES), 1)

    for j in range(blocks):
        cols = pl.ds(j * LANES, LANES)
        surface[j, 0:PAD, :] = above_ref[:, cols]
        surface[j, top:bottom, :] = band_ref[:, cols]
        surface[j, bottom:total, :] = below_ref[:, cols]
    for r in range(0, total, 8):
        surface[blocks, r : r + 8, :] = jnp.where(
            lane < LANES // 2, right_ref[r : r + 8, :], left_ref[r : r + 8, :]
        )

    def refill():
        @pl.when(top_edge)
        def _():
            for j in range(blocks + 1):
                surface[j, top - 2 : top, :] = jnp.broadcast_to(surface[j, top : top + 1, :], (2, LANES))

        @pl.when(bottom_edge)
        def _():
            for j in range(blocks + 1):
                surface[j, bottom : bottom + 2, :] = jnp.broadcast_to(
                    surface[j, bottom - 1 : bottom, :], (2, LANES)
                )

        @pl.when(left_edge)
        def _():
            for r in range(8, total - 8, 8):
                first = jnp.broadcast_to(surface[0, r : r + 8, 0:1], (8, LANES))
                surface[blocks, r : r + 8, :] = jnp.where(
                    lane >= LANES // 2, first, surface[blocks, r : r + 8, :]
                )

        @pl.when(right_edge)
        def _():
            for r in range(8, total - 8, 8):
                last = jnp.broadcast_to(
                    surface[blocks - 1, r : r + 8, LANES - 1 : LANES], (8, LANES)
                )
                surface[blocks, r : r + 8, :] = jnp.where(
                    lane < LANES // 2, last, surface[blocks, r : r + 8, :]
                )

    def across(pieces):
        after = [pltpu.roll(p, LANES - 1, 1) for p in pieces]
        before = [pltpu.roll(p, 1, 1) for p in pieces]
        n = len(pieces)
        return [
            jnp.where(lane == LANES - 1, after[(j + 1) % n], after[j])
            - jnp.where(lane == 0, before[(j - 1) % n], before[j])
            for j in range(n)
        ]

    for _ in range(SWEEPS):
        refill()
        for r in range(8, total - 8, 8):
            here = [surface[j, r : r + 8, :] for j in range(blocks + 1)]
            wide_x = across(here)
            wide_y = [
                surface[j, r + 1 : r + 9, :] - surface[j, r - 1 : r + 7, :] for j in range(blocks + 1)
            ]
            inverse = [
                lax.rsqrt(1.0 + 0.25 * (x * x + y * y)) for x, y in zip(wide_x, wide_y)
            ]
            spread = across([x * w for x, w in zip(wide_x, inverse)])
            for j in range(blocks + 1):
                normal_y[j, r : r + 8, :] = wide_y[j] * inverse[j]
                partial[j, r : r + 8, :] = here[j] + (0.25 * FLOW_STEP) * spread[j]
        for r in range(8, total - 8, 8):
            for j in range(blocks + 1):
                surface[j, r : r + 8, :] = partial[j, r : r + 8, :] + (0.25 * FLOW_STEP) * (
                    normal_y[j, r + 1 : r + 9, :] - normal_y[j, r - 1 : r + 7, :]
                )

    refill()
    for r in range(0, rows, 8):
        here = [surface[j, top + r : top + r + 8, :] for j in range(blocks + 1)]
        wide_x = across(here)
        for j in range(blocks):
            cols = pl.ds(j * LANES, LANES)
            x = 0.5 * wide_x[j]
            y = 0.5 * (
                surface[j, top + r + 1 : top + r + 9, :] - surface[j, top + r - 1 : top + r + 7, :]
            )
            inverse = lax.rsqrt(1.0 + (x * x + y * y))
            diffuse = jnp.maximum((0.8 - 0.36 * x - 0.48 * y) * inverse, 0.0)
            gloss = jnp.maximum((0.9487 - 0.1897 * x - 0.253 * y) * inverse, 0.0)
            for _ in range(4):
                gloss = gloss * gloss
            layers = [parts_ref[k, r : r + 8, cols] for k in range(parts_ref.shape[0])]
            thick = functools.reduce(jnp.add, layers)
            fluid = cover_ref[r : r + 8, cols].astype(jnp.float32)
            lit = 0.15 + 0.7 * jnp.exp(-0.8 * thick) * diffuse + 0.4 * gloss
            smooth_ref[r : r + 8, cols] = here[j]
            shade_ref[r : r + 8, cols] = fluid * lit + (1.0 - fluid) * 0.05


def local(depth_layers, thickness_layers, coverage):
    slabs = lax.axis_size("slab")
    grid = math.isqrt(lax.axis_size("tile"))
    slab = lax.axis_index("slab")
    tile = lax.axis_index("tile")
    _, _, height, width = depth_layers.shape
    rows = height // slabs
    core = slab % 2

    depth, thick = pair_cores(
        depth_layers.reshape(slabs, rows, width), thickness_layers.reshape(slabs, rows, width)
    )
    parts = to_owners(depth)
    thick = to_owners_by_swaps(thick, slab)[None]
    band = jnp.min(parts, axis=0)
    far, near = neighbour_rows(band, grid, slabs, core)
    odd = core == 1
    above, below = jnp.where(odd, near, far), jnp.where(odd, far, near)
    tall = [
        jnp.concatenate([a[:, cut] for a in (above, band, below)], axis=0)
        for cut in (slice(0, LANES), slice(width - LANES, width))
    ]
    left, right = neighbour_columns(*tall, grid, tile % grid)

    vmem = pl.BlockSpec(memory_space=pltpu.VMEM)
    total = rows + 2 * PAD
    blocks = width // LANES + 1
    out = jax.ShapeDtypeStruct((rows, width), jnp.float32)
    operands = [
        pltpu.with_memory_space_constraint(a, pltpu.VMEM) for a in (above, band, below, left, right, thick)
    ]
    smooth, shade = pl.pallas_call(
        functools.partial(flow_kernel, rows, width, grid, slabs),
        compiler_params=PARAMS,
        out_shape=(out, out),
        in_specs=[vmem] * 7,
        out_specs=(vmem, vmem),
        scratch_shapes=[pltpu.VMEM((blocks, total, LANES), jnp.float32)] * 3,
    )(*operands, coverage[0])
    return (smooth[None], shade[None])


def solution(mesh):
    return jax.shard_map(
        local,
        mesh=mesh,
        in_specs=(
            P("slab", "tile", None, None),
            P("slab", "tile", None, None),
            P("tile", "slab", None),
        ),
        out_specs=(P("tile", "slab", None), P("tile", "slab", None)),
        check_vma=False,
    )
```

```python
import functools
import math

import jax
import jax.numpy as jnp
from jax import lax
from jax.experimental import pallas as pl
from jax.experimental.pallas import tpu as pltpu
from jax.sharding import PartitionSpec as P

SWEEPS = 4
FLOW_STEP = 0.2

PAD = 16
LANES = 128
PARAMS = pltpu.CompilerParams(vmem_limit_bytes=16 * 1024 * 1024)


def pick_kernel(flip, value_ref, out_ref, sem):
    copy = pltpu.make_async_copy(
        value_ref.at[:, (lax.axis_index("slab") + flip) % 2], out_ref, sem
    )
    copy.start()
    copy.wait()


def pair_sum(value):
    bands, rows, width = value.shape
    value = value.reshape(bands // 2, 2, rows, width)
    value = pltpu.with_memory_space_constraint(value, pltpu.HBM)

    def pick(flip):
        return pl.pallas_call(
            functools.partial(pick_kernel, flip),
            compiler_params=PARAMS,
            out_shape=pltpu.VMEM((bands // 2, rows, width), jnp.float32),
            in_specs=[pl.BlockSpec(memory_space=pltpu.HBM)],
            out_specs=pl.BlockSpec(memory_space=pltpu.VMEM),
            scratch_shapes=[pltpu.SemaphoreType.DMA],
        )(value)

    own = pick(0)
    return own + lax.ppermute(pick(1), "slab", [(i, i ^ 1) for i in range(bands)])


def sum_by_swaps(value, slab):
    slabs = lax.axis_size("slab")
    chips = slabs // 2
    chip = slab // 2

    def share(index):
        return lax.dynamic_index_in_dim(value, index, 0, keepdims=False)

    total = share(chip)
    for step in range(1, chips):
        route = [(i, (i // 2 ^ step) * 2 + i % 2) for i in range(slabs)]
        total = total + lax.ppermute(share(chip ^ step), "slab", route)
    return total


def neighbour_rows(band, grid, slabs, core):
    tiles = grid * grid
    across = []
    for t in range(tiles):
        for s in range(1, slabs, 2):
            upper = s * tiles + t
            lower = (s + 1) * tiles + t if s + 1 < slabs else t + grid
            if s + 1 < slabs or t + grid < tiles:
                across += [(upper, lower), (lower, upper)]
    odd = core == 1
    head, tail = band[:PAD], band[-PAD:]
    long = jnp.where(odd, band[-PAD - 8 :], band[: PAD + 8])
    far = lax.ppermute(long, ("slab", "tile"), across)
    far = jnp.where(odd, far[:PAD], far[8:])
    near = lax.ppermute(jnp.where(odd, head, tail), "slab", [(i, i ^ 1) for i in range(slabs)])
    return far, near


def neighbour_columns(first, last, grid, column):
    odd = column % 2 == 1
    near, far = [], []
    for t in range(grid * grid):
        if t % grid + 1 < grid:
            (near if t % 2 == 0 else far).extend([(t, t + 1), (t + 1, t)])
    long = jnp.where(odd, last, first)
    long = jnp.concatenate([long, long[:8]], axis=0)
    far = lax.ppermute(long, "tile", far)[:-8]
    near = lax.ppermute(jnp.where(odd, first, last), "tile", near)
    return jnp.where(odd, near, far), jnp.where(odd, far, near)


def flow(rows, grid, pieces, last, first, groups, surface, partial, normal_y, finish):
    total = rows + 2 * PAD
    top, bottom = PAD, PAD + rows
    slabs = lax.axis_size("slab")
    slab, tile = lax.axis_index("slab"), lax.axis_index("tile")
    top_edge = (slab == 0) & (tile < grid)
    bottom_edge = (slab == slabs - 1) & (tile >= grid * (grid - 1))
    left_edge = lax.rem(tile, grid) == 0
    right_edge = lax.rem(tile, grid) == grid - 1
    lane = lax.broadcasted_iota(jnp.int32, (8, LANES), 1)
    first_row = lax.broadcasted_iota(jnp.int32, (8, LANES), 0) == 0
    last_row = lax.broadcasted_iota(jnp.int32, (8, LANES), 0) == 7
    first_lane, last_lane = lane == 0, lane == LANES - 1

    def across(values, left, right):
        after = [pltpu.roll(p, LANES - 1, 1) for p in values]
        before = [pltpu.roll(p, 1, 1) for p in values]
        out = []
        for j in range(pieces):
            beyond, behind = after[(j + 1) % pieces], before[(j - 1) % pieces]
            if j == first:
                behind = jnp.where(left_edge, left, behind)
            if j == last:
                beyond = jnp.where(right_edge, right, beyond)
            out.append(jnp.where(last_lane, beyond, after[j]) - jnp.where(first_lane, behind, before[j]))
        return out

    def slopes(r):
        here = [surface[j, pl.ds(r, 8), :] for j in range(pieces)]
        wide_x = across(here, here[first], here[last])
        at_top = first_row & (top_edge & (r == top))
        at_bottom = last_row & (bottom_edge & (r == bottom - 8))
        wide_y = []
        for j in range(pieces):
            over = jnp.where(at_top, here[j], surface[j, pl.ds(r - 1, 8), :])
            under = jnp.where(at_bottom, here[j], surface[j, pl.ds(r + 1, 8), :])
            wide_y.append(under - over)
        return here, wide_x, wide_y

    zero = jnp.zeros((8, LANES), jnp.float32)

    def bend(r):
        here, wide_x, wide_y = slopes(r)
        inverse = [lax.rsqrt(1.0 + 0.25 * (x * x + y * y)) for x, y in zip(wide_x, wide_y)]
        spread = across([x * w for x, w in zip(wide_x, inverse)], zero, zero)
        level = (top_edge & (r < top)) | (bottom_edge & (r >= bottom))
        for j in range(pieces):
            normal_y[j, pl.ds(r, 8), :] = jnp.where(level, 0.0, wide_y[j] * inverse[j])
            partial[j, pl.ds(r, 8), :] = here[j] + (0.25 * FLOW_STEP) * spread[j]

    def move(r):
        for j in range(pieces):
            surface[j, pl.ds(r, 8), :] = partial[j, pl.ds(r, 8), :] + (0.25 * FLOW_STEP) * (
                normal_y[j, pl.ds(r + 1, 8), :] - normal_y[j, pl.ds(r - 1, 8), :]
            )

    def each(start, count, group, act):
        def step(i, carry):
            for k in range(group):
                act(start + pl.multiple_of((i * group + k) * 8, 8))
            return carry

        lax.fori_loop(0, count // group, step, 0)

    def sweep(i, carry):
        each(8, total // 8 - 2, groups[0], bend)
        each(8, total // 8 - 2, groups[1], move)
        return carry

    lax.fori_loop(0, SWEEPS, sweep, 0)
    each(0, rows // 8, groups[2], lambda r: finish(r, *slopes(top + r)))


def shaded(wide_x, wide_y, layers, cover):
    x, y = 0.5 * wide_x, 0.5 * wide_y
    inverse = lax.rsqrt(1.0 + (x * x + y * y))
    diffuse = jnp.maximum((0.8 - 0.36 * x - 0.48 * y) * inverse, 0.0)
    gloss = jnp.maximum((0.9487 - 0.1897 * x - 0.253 * y) * inverse, 0.0)
    for _ in range(4):
        gloss = gloss * gloss
    fluid = cover.astype(jnp.float32)
    lit = 0.15 + 0.7 * jnp.exp(-0.8 * functools.reduce(jnp.add, layers)) * diffuse + 0.4 * gloss
    return fluid * lit + (1.0 - fluid) * 0.05


def inner_kernel(rows, grid, above_ref, band_ref, below_ref, thick_ref, cover_ref, smooth_ref, shade_ref, *scratch):
    surface = scratch[0]
    blocks = surface.shape[0]
    for j in range(blocks):
        cols = pl.ds(j * LANES, LANES)
        surface[j, 0:PAD, :] = above_ref[:, cols]
        surface[j, PAD : PAD + rows, :] = band_ref[:, cols]
        surface[j, PAD + rows :, :] = below_ref[:, cols]

    def finish(r, here, wide_x, wide_y):
        span = pl.ds(r, 8)
        for j in range(blocks):
            cols = pl.ds(j * LANES, LANES)
            smooth_ref[span, cols] = here[j]
            shade_ref[span, cols] = shaded(wide_x[j], wide_y[j], [thick_ref[span, cols]], cover_ref[span, cols])

    flow(rows, grid, blocks, blocks - 1, 0, (5, 10, 4), *scratch, finish)


def outer_kernel(
    rows,
    grid,
    above_ref,
    band_ref,
    below_ref,
    left_ref,
    right_ref,
    thick_ref,
    cover_ref,
    inner_smooth_ref,
    inner_shade_ref,
    smooth_ref,
    shade_ref,
    *scratch,
):
    surface = scratch[0]
    total = rows + 2 * PAD
    blocks = band_ref.shape[1] // LANES
    low = lax.broadcasted_iota(jnp.int32, (8, LANES), 1) < LANES // 2
    outer = ((0, blocks - 1), (2, 0))
    for j, block in outer:
        cols = pl.ds(block * LANES, LANES)
        surface[j, 0:PAD, :] = above_ref[:, cols]
        surface[j, PAD : PAD + rows, :] = band_ref[:, cols]
        surface[j, PAD + rows :, :] = below_ref[:, cols]
    for r in range(0, total, 8):
        surface[1, r : r + 8, :] = jnp.where(low, right_ref[r : r + 8, :], left_ref[r : r + 8, :])
    middle = pl.ds(LANES, (blocks - 2) * LANES)
    smooth_ref[:, middle] = inner_smooth_ref[:, middle]
    shade_ref[:, middle] = inner_shade_ref[:, middle]

    def finish(r, here, wide_x, wide_y):
        span = pl.ds(r, 8)
        for j, block in outer:
            cols = pl.ds(block * LANES, LANES)
            keep = low if j == 0 else jnp.logical_not(low)
            shade = shaded(wide_x[j], wide_y[j], [thick_ref[span, cols]], cover_ref[span, cols])
            smooth_ref[span, cols] = jnp.where(keep, inner_smooth_ref[span, cols], here[j])
            shade_ref[span, cols] = jnp.where(keep, inner_shade_ref[span, cols], shade)

    flow(rows, grid, 3, 0, 2, (10, 10, 8), *scratch, finish)


def local(depth_layers, thickness_layers, coverage):
    slabs = lax.axis_size("slab")
    grid = math.isqrt(lax.axis_size("tile"))
    slab = lax.axis_index("slab")
    tile = lax.axis_index("tile")
    _, _, height, width = depth_layers.shape
    rows = height // slabs
    core = slab % 2

    parts = lax.all_to_all(
        depth_layers.reshape(slabs, rows, width), "slab", split_axis=0, concat_axis=0, tiled=True
    )
    thick = sum_by_swaps(pair_sum(thickness_layers.reshape(slabs, rows, width)), slab)
    band = jnp.min(parts, axis=0)
    far, near = neighbour_rows(band, grid, slabs, core)
    odd = core == 1
    above, below = jnp.where(odd, near, far), jnp.where(odd, far, near)
    tall = [
        jnp.concatenate([a[:, cut] for a in (above, band, below)], axis=0)
        for cut in (slice(0, LANES), slice(width - LANES, width))
    ]
    left, right = neighbour_columns(*tall, grid, tile % grid)

    vmem = pl.BlockSpec(memory_space=pltpu.VMEM)
    total = rows + 2 * PAD
    blocks = width // LANES
    above, band, below, left, right, thick, cover = (
        pltpu.with_memory_space_constraint(a, pltpu.VMEM)
        for a in (above, band, below, left, right, thick, coverage[0])
    )
    held = pltpu.VMEM((rows, width), jnp.float32)
    inner = pl.pallas_call(
        functools.partial(inner_kernel, rows, grid),
        compiler_params=PARAMS,
        out_shape=(held, held),
        in_specs=[vmem] * 5,
        out_specs=(vmem, vmem),
        scratch_shapes=[pltpu.VMEM((blocks, total, LANES), jnp.float32)] * 3,
    )(above, band, below, thick, cover)
    out = jax.ShapeDtypeStruct((rows, width), jnp.float32)
    smooth, shade = pl.pallas_call(
        functools.partial(outer_kernel, rows, grid),
        compiler_params=PARAMS,
        out_shape=(out, out),
        in_specs=[vmem] * 9,
        out_specs=(vmem, vmem),
        scratch_shapes=[pltpu.VMEM((3, total, LANES), jnp.float32)] * 3,
    )(
        above,
        band,
        below,
        left,
        right,
        thick,
        cover,
        *(pltpu.with_memory_space_constraint(a, pltpu.VMEM) for a in inner),
    )
    return (smooth[None], shade[None])


def solution(mesh):
    return jax.shard_map(
        local,
        mesh=mesh,
        in_specs=(
            P("slab", "tile", None, None),
            P("slab", "tile", None, None),
            P("tile", "slab", None),
        ),
        out_specs=(P("tile", "slab", None), P("tile", "slab", None)),
        check_vma=False,
    )
```

```python
import functools
import math

import jax
import jax.numpy as jnp
from jax import lax
from jax.experimental import pallas as pl
from jax.experimental.pallas import tpu as pltpu
from jax.sharding import PartitionSpec as P

SWEEPS = 4
FLOW_STEP = 0.2

PAD = 16
LANES = 128
PARAMS = pltpu.CompilerParams(vmem_limit_bytes=16 * 1024 * 1024)


def pick_kernel(flip, value_ref, out_ref, sem):
    copy = pltpu.make_async_copy(
        value_ref.at[:, (lax.axis_index("slab") + flip) % 2], out_ref, sem
    )
    copy.start()
    copy.wait()


def pair_sum(value):
    bands, rows, width = value.shape
    value = value.reshape(bands // 2, 2, rows, width)
    value = pltpu.with_memory_space_constraint(value, pltpu.HBM)

    def pick(flip):
        return pl.pallas_call(
            functools.partial(pick_kernel, flip),
            compiler_params=PARAMS,
            out_shape=pltpu.VMEM((bands // 2, rows, width), jnp.float32),
            in_specs=[pl.BlockSpec(memory_space=pltpu.HBM)],
            out_specs=pl.BlockSpec(memory_space=pltpu.VMEM),
            scratch_shapes=[pltpu.SemaphoreType.DMA],
        )(value)

    own = pick(0)
    return own + lax.ppermute(pick(1), "slab", [(i, i ^ 1) for i in range(bands)])


def sum_by_swaps(value, slab):
    slabs = lax.axis_size("slab")
    chips = slabs // 2
    chip = slab // 2

    def share(index):
        return lax.dynamic_index_in_dim(value, index, 0, keepdims=False)

    total = share(chip)
    for step in range(1, chips):
        route = [(i, (i // 2 ^ step) * 2 + i % 2) for i in range(slabs)]
        total = total + lax.ppermute(share(chip ^ step), "slab", route)
    return total


def neighbour_rows(band, grid, slabs, core):
    tiles = grid * grid
    across = []
    for t in range(tiles):
        for s in range(1, slabs, 2):
            upper = s * tiles + t
            lower = (s + 1) * tiles + t if s + 1 < slabs else t + grid
            if s + 1 < slabs or t + grid < tiles:
                across += [(upper, lower), (lower, upper)]
    odd = core == 1
    head, tail = band[:PAD], band[-PAD:]
    long = jnp.where(odd, band[-PAD - 8 :], band[: PAD + 8])
    far = lax.ppermute(long, ("slab", "tile"), across)
    far = jnp.where(odd, far[:PAD], far[8:])
    near = lax.ppermute(jnp.where(odd, head, tail), "slab", [(i, i ^ 1) for i in range(slabs)])
    return far, near


def pack(block, start):
    size = block.shape[0] // 4
    return jnp.concatenate(
        [block[k * size : (k + 1) * size, start : start + LANES // 4] for k in range(4)], axis=1
    )


def neighbour_columns(first, last, grid, column):
    odd = column % 2 == 1
    near, far = [], []
    for t in range(grid * grid):
        if t % grid + 1 < grid:
            (near if t % 2 == 0 else far).extend([(t, t + 1), (t + 1, t)])
    first, last = pack(first, 0), pack(last, LANES - LANES // 4)
    long = jnp.where(odd, last, first)
    long = jnp.concatenate([long, long[:8]], axis=0)
    far = lax.ppermute(long, "tile", far)[:-8]
    near = lax.ppermute(jnp.where(odd, first, last), "tile", near)
    return jnp.where(odd, near, far), jnp.where(odd, far, near)


def flow(rows, grid, pieces, last, first, groups, surface, partial, normal_y, finish):
    total = rows + 2 * PAD
    top, bottom = PAD, PAD + rows
    slabs = lax.axis_size("slab")
    slab, tile = lax.axis_index("slab"), lax.axis_index("tile")
    top_edge = (slab == 0) & (tile < grid)
    bottom_edge = (slab == slabs - 1) & (tile >= grid * (grid - 1))
    left_edge = lax.rem(tile, grid) == 0
    right_edge = lax.rem(tile, grid) == grid - 1
    lane = lax.broadcasted_iota(jnp.int32, (8, LANES), 1)
    first_row = lax.broadcasted_iota(jnp.int32, (8, LANES), 0) == 0
    last_row = lax.broadcasted_iota(jnp.int32, (8, LANES), 0) == 7
    first_lane, last_lane = lane == 0, lane == LANES - 1
    at_left, at_right = left_edge & (lane == first[1]), right_edge & (lane == last[1])

    def across(values, left, right):
        after = [pltpu.roll(p, LANES - 1, 1) for p in values]
        before = [pltpu.roll(p, 1, 1) for p in values]
        out = []
        for j in range(pieces):
            beyond, behind = after[j], before[j]
            if pieces > 1:
                beyond = jnp.where(last_lane, after[(j + 1) % pieces], beyond)
                behind = jnp.where(first_lane, before[(j - 1) % pieces], behind)
            if j == last[0]:
                beyond = jnp.where(at_right, right, beyond)
            if j == first[0]:
                behind = jnp.where(at_left, left, behind)
            out.append(beyond - behind)
        return out

    def slopes(r):
        here = [surface[j, pl.ds(r, 8), :] for j in range(pieces)]
        wide_x = across(here, here[first[0]], here[last[0]])
        at_top = first_row & (top_edge & (r == top))
        at_bottom = last_row & (bottom_edge & (r == bottom - 8))
        wide_y = []
        for j in range(pieces):
            over = jnp.where(at_top, here[j], surface[j, pl.ds(r - 1, 8), :])
            under = jnp.where(at_bottom, here[j], surface[j, pl.ds(r + 1, 8), :])
            wide_y.append(under - over)
        return here, wide_x, wide_y

    zero = jnp.zeros((8, LANES), jnp.float32)

    def bend(r):
        here, wide_x, wide_y = slopes(r)
        inverse = [lax.rsqrt(1.0 + 0.25 * (x * x + y * y)) for x, y in zip(wide_x, wide_y)]
        spread = across([x * w for x, w in zip(wide_x, inverse)], zero, zero)
        level = (top_edge & (r < top)) | (bottom_edge & (r >= bottom))
        for j in range(pieces):
            normal_y[j, pl.ds(r, 8), :] = jnp.where(level, 0.0, wide_y[j] * inverse[j])
            partial[j, pl.ds(r, 8), :] = here[j] + (0.25 * FLOW_STEP) * spread[j]

    def move(r):
        for j in range(pieces):
            surface[j, pl.ds(r, 8), :] = partial[j, pl.ds(r, 8), :] + (0.25 * FLOW_STEP) * (
                normal_y[j, pl.ds(r + 1, 8), :] - normal_y[j, pl.ds(r - 1, 8), :]
            )

    def each(start, count, group, act):
        def step(i, carry):
            for k in range(group):
                act(start + pl.multiple_of((i * group + k) * 8, 8))
            return carry

        lax.fori_loop(0, count // group, step, 0)

    def sweep(i, carry):
        each(8, total // 8 - 2, groups[0], bend)
        each(8, total // 8 - 2, groups[1], move)
        return carry

    lax.fori_loop(0, SWEEPS, sweep, 0)
    each(0, rows // 8, groups[2], lambda r: finish(r, *slopes(top + r)))


def shaded(wide_x, wide_y, layers, cover):
    x, y = 0.5 * wide_x, 0.5 * wide_y
    inverse = lax.rsqrt(1.0 + (x * x + y * y))
    diffuse = jnp.maximum((0.8 - 0.36 * x - 0.48 * y) * inverse, 0.0)
    gloss = jnp.maximum((0.9487 - 0.1897 * x - 0.253 * y) * inverse, 0.0)
    for _ in range(4):
        gloss = gloss * gloss
    fluid = cover.astype(jnp.float32)
    lit = 0.15 + 0.7 * jnp.exp(-0.8 * functools.reduce(jnp.add, layers)) * diffuse + 0.4 * gloss
    return fluid * lit + (1.0 - fluid) * 0.05


def inner_kernel(rows, grid, above_ref, band_ref, below_ref, thick_ref, cover_ref, smooth_ref, shade_ref, *scratch):
    surface = scratch[0]
    blocks = surface.shape[0]
    for j in range(blocks):
        cols = pl.ds(j * LANES, LANES)
        surface[j, 0:PAD, :] = above_ref[:, cols]
        surface[j, PAD : PAD + rows, :] = band_ref[:, cols]
        surface[j, PAD + rows :, :] = below_ref[:, cols]

    def finish(r, here, wide_x, wide_y):
        span = pl.ds(r, 8)
        for j in range(blocks):
            cols = pl.ds(j * LANES, LANES)
            smooth_ref[span, cols] = here[j]
            shade_ref[span, cols] = shaded(wide_x[j], wide_y[j], [thick_ref[span, cols]], cover_ref[span, cols])

    flow(rows, grid, blocks, (blocks - 1, LANES - 1), (0, 0), (5, 10, 4), *scratch, finish)


def outer_kernel(
    rows,
    grid,
    above_ref,
    band_ref,
    below_ref,
    left_ref,
    right_ref,
    thick_ref,
    cover_ref,
    inner_smooth_ref,
    inner_shade_ref,
    smooth_ref,
    shade_ref,
    *scratch,
):
    surface = scratch[0]
    total = rows + 2 * PAD
    blocks = band_ref.shape[1] // LANES
    quarter = LANES // 4
    lane = lax.broadcasted_iota(jnp.int32, (8, LANES), 1)
    low = lane < LANES // 2

    def own(r, block):
        cols = pl.ds(block * LANES, LANES)
        if r < PAD:
            return above_ref[r : r + 8, cols]
        if r < PAD + rows:
            return band_ref[r - PAD : r - PAD + 8, cols]
        return below_ref[r - PAD - rows : r - PAD - rows + 8, cols]

    size = total // 4
    for r in range(0, total, 8):
        group, row = r // size, r % size
        right = pltpu.roll(right_ref[row : row + 8, :], (5 - group) % 4 * quarter, 1)
        left = pltpu.roll(left_ref[row : row + 8, :], (6 - group) % 4 * quarter, 1)
        at_right = jnp.where(lane < quarter, pltpu.roll(own(r, blocks - 1), quarter, 1), right)
        at_left = jnp.where(lane < 3 * quarter, left, pltpu.roll(own(r, 0), 3 * quarter, 1))
        surface[0, r : r + 8, :] = jnp.where(low, at_right, at_left)
    middle = pl.ds(LANES, (blocks - 2) * LANES)
    smooth_ref[:, middle] = inner_smooth_ref[:, middle]
    shade_ref[:, middle] = inner_shade_ref[:, middle]
    outer = (
        (0, quarter, lane < quarter // 2),
        (blocks - 1, 3 * quarter, lane >= LANES - quarter // 2),
    )

    def finish(r, here, wide_x, wide_y):
        span = pl.ds(r, 8)
        for block, shift, new in outer:
            cols = pl.ds(block * LANES, LANES)
            smooth, x, y = (pltpu.roll(a[0], shift, 1) for a in (here, wide_x, wide_y))
            shade = shaded(x, y, [thick_ref[span, cols]], cover_ref[span, cols])
            smooth_ref[span, cols] = jnp.where(new, smooth, inner_smooth_ref[span, cols])
            shade_ref[span, cols] = jnp.where(new, shade, inner_shade_ref[span, cols])

    flow(rows, grid, 1, (0, quarter - 1), (0, 3 * quarter), (10, 10, 8), *scratch, finish)


def local(depth_layers, thickness_layers, coverage):
    slabs = lax.axis_size("slab")
    grid = math.isqrt(lax.axis_size("tile"))
    slab = lax.axis_index("slab")
    tile = lax.axis_index("tile")
    _, _, height, width = depth_layers.shape
    rows = height // slabs
    core = slab % 2

    parts = lax.all_to_all(
        depth_layers.reshape(slabs, rows, width), "slab", split_axis=0, concat_axis=0, tiled=True
    )
    thick = sum_by_swaps(pair_sum(thickness_layers.reshape(slabs, rows, width)), slab)
    band = jnp.min(parts, axis=0)
    far, near = neighbour_rows(band, grid, slabs, core)
    odd = core == 1
    above, below = jnp.where(odd, near, far), jnp.where(odd, far, near)
    tall = [
        jnp.concatenate([a[:, cut] for a in (above, band, below)], axis=0)
        for cut in (slice(0, LANES), slice(width - LANES, width))
    ]
    left, right = neighbour_columns(*tall, grid, tile % grid)

    vmem = pl.BlockSpec(memory_space=pltpu.VMEM)
    total = rows + 2 * PAD
    blocks = width // LANES
    above, band, below, left, right, thick, cover = (
        pltpu.with_memory_space_constraint(a, pltpu.VMEM)
        for a in (above, band, below, left, right, thick, coverage[0])
    )
    held = pltpu.VMEM((rows, width), jnp.float32)
    inner = pl.pallas_call(
        functools.partial(inner_kernel, rows, grid),
        compiler_params=PARAMS,
        out_shape=(held, held),
        in_specs=[vmem] * 5,
        out_specs=(vmem, vmem),
        scratch_shapes=[pltpu.VMEM((blocks, total, LANES), jnp.float32)] * 3,
    )(above, band, below, thick, cover)
    out = jax.ShapeDtypeStruct((rows, width), jnp.float32)
    smooth, shade = pl.pallas_call(
        functools.partial(outer_kernel, rows, grid),
        compiler_params=PARAMS,
        out_shape=(out, out),
        in_specs=[vmem] * 9,
        out_specs=(vmem, vmem),
        scratch_shapes=[pltpu.VMEM((1, total, LANES), jnp.float32)] * 3,
    )(
        above,
        band,
        below,
        left,
        right,
        thick,
        cover,
        *(pltpu.with_memory_space_constraint(a, pltpu.VMEM) for a in inner),
    )
    return (smooth[None], shade[None])


def solution(mesh):
    return jax.shard_map(
        local,
        mesh=mesh,
        in_specs=(
            P("slab", "tile", None, None),
            P("slab", "tile", None, None),
            P("tile", "slab", None),
        ),
        out_specs=(P("tile", "slab", None), P("tile", "slab", None)),
        check_vma=False,
    )
```

```python
import functools
import math

import jax
import jax.numpy as jnp
from jax import lax
from jax.experimental import pallas as pl
from jax.experimental.pallas import tpu as pltpu
from jax.sharding import PartitionSpec as P

SWEEPS = 4
FLOW_STEP = 0.2

PAD = 16
LANES = 128
PARAMS = pltpu.CompilerParams(vmem_limit_bytes=16 * 1024 * 1024)


def pick_kernel(flip, value_ref, out_ref, sem):
    copy = pltpu.make_async_copy(
        value_ref.at[:, (lax.axis_index("slab") + flip) % 2], out_ref, sem
    )
    copy.start()
    copy.wait()


def pair_sum(value):
    bands, rows, width = value.shape
    value = value.reshape(bands // 2, 2, rows, width)
    value = pltpu.with_memory_space_constraint(value, pltpu.HBM)

    def pick(flip):
        return pl.pallas_call(
            functools.partial(pick_kernel, flip),
            compiler_params=PARAMS,
            out_shape=pltpu.VMEM((bands // 2, rows, width), jnp.float32),
            in_specs=[pl.BlockSpec(memory_space=pltpu.HBM)],
            out_specs=pl.BlockSpec(memory_space=pltpu.VMEM),
            scratch_shapes=[pltpu.SemaphoreType.DMA],
        )(value)

    own = pick(0)
    return own + lax.ppermute(pick(1), "slab", [(i, i ^ 1) for i in range(bands)])


def sum_by_swaps(value, slab):
    slabs = lax.axis_size("slab")
    chips = slabs // 2
    chip = slab // 2

    def share(index):
        return lax.dynamic_index_in_dim(value, index, 0, keepdims=False)

    total = share(chip)
    for step in (3, 2, 1):
        route = [(i, (i // 2 ^ step) * 2 + i % 2) for i in range(slabs)]
        total = total + lax.ppermute(share(chip ^ step), "slab", route)
    return total


def neighbour_rows(band, grid, slabs, core):
    tiles = grid * grid
    across = []
    for t in range(tiles):
        for s in range(1, slabs, 2):
            upper = s * tiles + t
            lower = (s + 1) * tiles + t if s + 1 < slabs else t + grid
            if s + 1 < slabs or t + grid < tiles:
                across += [(upper, lower), (lower, upper)]
    odd = core == 1
    head, tail = band[:PAD], band[-PAD:]
    long = jnp.where(odd, band[-PAD - 8 :], band[: PAD + 8])
    far = lax.ppermute(long, ("slab", "tile"), across)
    far = jnp.where(odd, far[:PAD], far[8:])
    near = lax.ppermute(jnp.where(odd, head, tail), "slab", [(i, i ^ 1) for i in range(slabs)])
    return far, near


def pack(block, start):
    size = block.shape[0] // 4
    return jnp.concatenate(
        [block[k * size : (k + 1) * size, start : start + LANES // 4] for k in range(4)], axis=1
    )


def neighbour_columns(first, last, grid, column):
    odd = column % 2 == 1
    near, far = [], []
    for t in range(grid * grid):
        if t % grid + 1 < grid:
            (near if t % 2 == 0 else far).extend([(t, t + 1), (t + 1, t)])
    first, last = pack(first, 0), pack(last, LANES - LANES // 4)
    long = jnp.where(odd, last, first)
    long = jnp.concatenate([long, long[:8]], axis=0)
    far = lax.ppermute(long, "tile", far)[:-8]
    near = lax.ppermute(jnp.where(odd, first, last), "tile", near)
    return jnp.where(odd, near, far), jnp.where(odd, far, near)


def flow(rows, grid, pieces, last, first, groups, surface, partial, normal_y, finish):
    total = rows + 2 * PAD
    top, bottom = PAD, PAD + rows
    slabs = lax.axis_size("slab")
    slab, tile = lax.axis_index("slab"), lax.axis_index("tile")
    top_edge = (slab == 0) & (tile < grid)
    bottom_edge = (slab == slabs - 1) & (tile >= grid * (grid - 1))
    left_edge = lax.rem(tile, grid) == 0
    right_edge = lax.rem(tile, grid) == grid - 1
    lane = lax.broadcasted_iota(jnp.int32, (8, LANES), 1)
    first_row = lax.broadcasted_iota(jnp.int32, (8, LANES), 0) == 0
    last_row = lax.broadcasted_iota(jnp.int32, (8, LANES), 0) == 7
    first_lane, last_lane = lane == 0, lane == LANES - 1
    at_left, at_right = left_edge & (lane == first[1]), right_edge & (lane == last[1])

    def across(values, left, right):
        after = [pltpu.roll(p, LANES - 1, 1) for p in values]
        before = [pltpu.roll(p, 1, 1) for p in values]
        out = []
        for j in range(pieces):
            beyond, behind = after[j], before[j]
            if pieces > 1:
                beyond = jnp.where(last_lane, after[(j + 1) % pieces], beyond)
                behind = jnp.where(first_lane, before[(j - 1) % pieces], behind)
            if j == last[0]:
                beyond = jnp.where(at_right, right, beyond)
            if j == first[0]:
                behind = jnp.where(at_left, left, behind)
            out.append(beyond - behind)
        return out

    def slopes(r):
        here = [surface[j, pl.ds(r, 8), :] for j in range(pieces)]
        wide_x = across(here, here[first[0]], here[last[0]])
        at_top = first_row & (top_edge & (r == top))
        at_bottom = last_row & (bottom_edge & (r == bottom - 8))
        wide_y = []
        for j in range(pieces):
            over = jnp.where(at_top, here[j], surface[j, pl.ds(r - 1, 8), :])
            under = jnp.where(at_bottom, here[j], surface[j, pl.ds(r + 1, 8), :])
            wide_y.append(under - over)
        return here, wide_x, wide_y

    zero = jnp.zeros((8, LANES), jnp.float32)

    def bend(r):
        here, wide_x, wide_y = slopes(r)
        inverse = [lax.rsqrt(1.0 + 0.25 * (x * x + y * y)) for x, y in zip(wide_x, wide_y)]
        spread = across([x * w for x, w in zip(wide_x, inverse)], zero, zero)
        level = (top_edge & (r < top)) | (bottom_edge & (r >= bottom))
        for j in range(pieces):
            normal_y[j, pl.ds(r, 8), :] = jnp.where(level, 0.0, wide_y[j] * inverse[j])
            partial[j, pl.ds(r, 8), :] = here[j] + (0.25 * FLOW_STEP) * spread[j]

    def move(r):
        for j in range(pieces):
            surface[j, pl.ds(r, 8), :] = partial[j, pl.ds(r, 8), :] + (0.25 * FLOW_STEP) * (
                normal_y[j, pl.ds(r + 1, 8), :] - normal_y[j, pl.ds(r - 1, 8), :]
            )

    def each(start, count, group, act):
        def step(i, carry):
            for k in range(group):
                act(start + pl.multiple_of((i * group + k) * 8, 8))
            return carry

        lax.fori_loop(0, count // group, step, 0)

    def sweep(i, carry):
        each(8, total // 8 - 2, groups[0], bend)
        each(8, total // 8 - 2, groups[1], move)
        return carry

    lax.fori_loop(0, SWEEPS, sweep, 0)
    each(0, rows // 8, groups[2], lambda r: finish(r, *slopes(top + r)))


def shaded(wide_x, wide_y, layers, cover):
    x, y = 0.5 * wide_x, 0.5 * wide_y
    inverse = lax.rsqrt(1.0 + (x * x + y * y))
    diffuse = jnp.maximum((0.8 - 0.36 * x - 0.48 * y) * inverse, 0.0)
    gloss = jnp.maximum((0.9487 - 0.1897 * x - 0.253 * y) * inverse, 0.0)
    for _ in range(4):
        gloss = gloss * gloss
    fluid = cover.astype(jnp.float32)
    lit = 0.15 + 0.7 * jnp.exp(-0.8 * functools.reduce(jnp.add, layers)) * diffuse + 0.4 * gloss
    return fluid * lit + (1.0 - fluid) * 0.05


def inner_kernel(rows, grid, above_ref, band_ref, below_ref, thick_ref, cover_ref, smooth_ref, shade_ref, *scratch):
    surface = scratch[0]
    blocks = surface.shape[0]
    for j in range(blocks):
        cols = pl.ds(j * LANES, LANES)
        surface[j, 0:PAD, :] = above_ref[:, cols]
        surface[j, PAD : PAD + rows, :] = band_ref[:, cols]
        surface[j, PAD + rows :, :] = below_ref[:, cols]

    def finish(r, here, wide_x, wide_y):
        span = pl.ds(r, 8)
        for j in range(blocks):
            cols = pl.ds(j * LANES, LANES)
            smooth_ref[span, cols] = here[j]
            shade_ref[span, cols] = shaded(wide_x[j], wide_y[j], [thick_ref[span, cols]], cover_ref[span, cols])

    flow(rows, grid, blocks, (blocks - 1, LANES - 1), (0, 0), (5, 10, 4), *scratch, finish)


def outer_kernel(
    rows,
    grid,
    above_ref,
    band_ref,
    below_ref,
    left_ref,
    right_ref,
    thick_ref,
    cover_ref,
    inner_smooth_ref,
    inner_shade_ref,
    smooth_ref,
    shade_ref,
    *scratch,
):
    surface = scratch[0]
    total = rows + 2 * PAD
    blocks = band_ref.shape[1] // LANES
    quarter = LANES // 4
    lane = lax.broadcasted_iota(jnp.int32, (8, LANES), 1)
    low = lane < LANES // 2

    def own(r, block):
        cols = pl.ds(block * LANES, LANES)
        if r < PAD:
            return above_ref[r : r + 8, cols]
        if r < PAD + rows:
            return band_ref[r - PAD : r - PAD + 8, cols]
        return below_ref[r - PAD - rows : r - PAD - rows + 8, cols]

    size = total // 4
    for r in range(0, total, 8):
        group, row = r // size, r % size
        right = pltpu.roll(right_ref[row : row + 8, :], (5 - group) % 4 * quarter, 1)
        left = pltpu.roll(left_ref[row : row + 8, :], (6 - group) % 4 * quarter, 1)
        at_right = jnp.where(lane < quarter, pltpu.roll(own(r, blocks - 1), quarter, 1), right)
        at_left = jnp.where(lane < 3 * quarter, left, pltpu.roll(own(r, 0), 3 * quarter, 1))
        surface[0, r : r + 8, :] = jnp.where(low, at_right, at_left)
    middle = pl.ds(LANES, (blocks - 2) * LANES)
    smooth_ref[:, middle] = inner_smooth_ref[:, middle]
    shade_ref[:, middle] = inner_shade_ref[:, middle]
    outer = (
        (0, quarter, lane < quarter // 2),
        (blocks - 1, 3 * quarter, lane >= LANES - quarter // 2),
    )

    def finish(r, here, wide_x, wide_y):
        span = pl.ds(r, 8)
        for block, shift, new in outer:
            cols = pl.ds(block * LANES, LANES)
            smooth, x, y = (pltpu.roll(a[0], shift, 1) for a in (here, wide_x, wide_y))
            shade = shaded(x, y, [thick_ref[span, cols]], cover_ref[span, cols])
            smooth_ref[span, cols] = jnp.where(new, smooth, inner_smooth_ref[span, cols])
            shade_ref[span, cols] = jnp.where(new, shade, inner_shade_ref[span, cols])

    flow(rows, grid, 1, (0, quarter - 1), (0, 3 * quarter), (10, 10, 8), *scratch, finish)


def local(depth_layers, thickness_layers, coverage):
    slabs = lax.axis_size("slab")
    grid = math.isqrt(lax.axis_size("tile"))
    slab = lax.axis_index("slab")
    tile = lax.axis_index("tile")
    _, _, height, width = depth_layers.shape
    rows = height // slabs
    core = slab % 2

    parts = lax.all_to_all(
        depth_layers.reshape(slabs, rows, width), "slab", split_axis=0, concat_axis=0, tiled=True
    )
    thick = sum_by_swaps(pair_sum(thickness_layers.reshape(slabs, rows, width)), slab)
    band = jnp.min(parts, axis=0)
    far, near = neighbour_rows(band, grid, slabs, core)
    odd = core == 1
    above, below = jnp.where(odd, near, far), jnp.where(odd, far, near)
    tall = [
        jnp.concatenate([a[:, cut] for a in (above, band, below)], axis=0)
        for cut in (slice(0, LANES), slice(width - LANES, width))
    ]
    left, right = neighbour_columns(*tall, grid, tile % grid)

    vmem = pl.BlockSpec(memory_space=pltpu.VMEM)
    total = rows + 2 * PAD
    blocks = width // LANES
    above, band, below, left, right, thick, cover = (
        pltpu.with_memory_space_constraint(a, pltpu.VMEM)
        for a in (above, band, below, left, right, thick, coverage[0])
    )
    held = pltpu.VMEM((rows, width), jnp.float32)
    inner = pl.pallas_call(
        functools.partial(inner_kernel, rows, grid),
        compiler_params=PARAMS,
        out_shape=(held, held),
        in_specs=[vmem] * 5,
        out_specs=(vmem, vmem),
        scratch_shapes=[pltpu.VMEM((blocks, total, LANES), jnp.float32)] * 3,
    )(above, band, below, thick, cover)
    out = jax.ShapeDtypeStruct((rows, width), jnp.float32)
    smooth, shade = pl.pallas_call(
        functools.partial(outer_kernel, rows, grid),
        compiler_params=PARAMS,
        out_shape=(out, out),
        in_specs=[vmem] * 9,
        out_specs=(vmem, vmem),
        scratch_shapes=[pltpu.VMEM((1, total, LANES), jnp.float32)] * 3,
    )(
        above,
        band,
        below,
        left,
        right,
        thick,
        cover,
        *(pltpu.with_memory_space_constraint(a, pltpu.VMEM) for a in inner),
    )
    return (smooth[None], shade[None])


def solution(mesh):
    return jax.shard_map(
        local,
        mesh=mesh,
        in_specs=(
            P("slab", "tile", None, None),
            P("slab", "tile", None, None),
            P("tile", "slab", None),
        ),
        out_specs=(P("tile", "slab", None), P("tile", "slab", None)),
        check_vma=False,
    )
```

```python
import functools
import math

import jax
import jax.numpy as jnp
from jax import lax
from jax.experimental import pallas as pl
from jax.experimental.pallas import tpu as pltpu
from jax.sharding import PartitionSpec as P

SWEEPS = 4
FLOW_STEP = 0.2

PAD = 16
LANES = 128
PARAMS = pltpu.CompilerParams(vmem_limit_bytes=16 * 1024 * 1024)


def pick_kernel(flip, value_ref, out_ref, sem):
    copy = pltpu.make_async_copy(
        value_ref.at[:, (lax.axis_index("slab") + flip) % 2], out_ref, sem
    )
    copy.start()
    copy.wait()


def pair_sum(value):
    bands, rows, width = value.shape
    value = value.reshape(bands // 2, 2, rows, width)
    value = pltpu.with_memory_space_constraint(value, pltpu.HBM)

    def pick(flip):
        return pl.pallas_call(
            functools.partial(pick_kernel, flip),
            compiler_params=PARAMS,
            out_shape=pltpu.VMEM((bands // 2, rows, width), jnp.float32),
            in_specs=[pl.BlockSpec(memory_space=pltpu.HBM)],
            out_specs=pl.BlockSpec(memory_space=pltpu.VMEM),
            scratch_shapes=[pltpu.SemaphoreType.DMA],
        )(value)

    own = pick(0)
    return own + lax.ppermute(pick(1), "slab", [(i, i ^ 1) for i in range(bands)])


def sum_by_swaps(value, slab):
    slabs = lax.axis_size("slab")
    chips = slabs // 2
    chip = slab // 2

    def share(index):
        return lax.dynamic_index_in_dim(value, index, 0, keepdims=False)

    total = share(chip)
    for step in (3, 2, 1):
        route = [(i, (i // 2 ^ step) * 2 + i % 2) for i in range(slabs)]
        total = total + lax.ppermute(share(chip ^ step), "slab", route)
    return total


def neighbour_rows(band, grid, slabs, core):
    tiles = grid * grid
    across = []
    for t in range(tiles):
        for s in range(1, slabs, 2):
            upper = s * tiles + t
            lower = (s + 1) * tiles + t if s + 1 < slabs else t + grid
            if s + 1 < slabs or t + grid < tiles:
                across += [(upper, lower), (lower, upper)]
    odd = core == 1
    head, tail = band[:PAD], band[-PAD:]
    long = jnp.where(odd, tail, head)
    long = jnp.concatenate([long, long[:, :LANES]], axis=1)
    far = lax.ppermute(long, ("slab", "tile"), across)[:, :-LANES]
    near = lax.ppermute(jnp.where(odd, head, tail), "slab", [(i, i ^ 1) for i in range(slabs)])
    return far, near


def pack(block, start):
    size = block.shape[0] // 4
    return jnp.concatenate(
        [block[k * size : (k + 1) * size, start : start + LANES // 4] for k in range(4)], axis=1
    )


def neighbour_columns(first, last, grid, column):
    odd = column % 2 == 1
    near, far = [], []
    for t in range(grid * grid):
        if t % grid + 1 < grid:
            (near if t % 2 == 0 else far).extend([(t, t + 1), (t + 1, t)])
    first, last = pack(first, 0), pack(last, LANES - LANES // 4)
    long = jnp.where(odd, last, first)
    long = jnp.concatenate([long, long[:8]], axis=0)
    far = lax.ppermute(long, "tile", far)[:-8]
    near = lax.ppermute(jnp.where(odd, first, last), "tile", near)
    return jnp.where(odd, near, far), jnp.where(odd, far, near)


def flow(rows, grid, pieces, last, first, groups, surface, partial, normal_y, finish):
    total = rows + 2 * PAD
    top, bottom = PAD, PAD + rows
    slabs = lax.axis_size("slab")
    slab, tile = lax.axis_index("slab"), lax.axis_index("tile")
    top_edge = (slab == 0) & (tile < grid)
    bottom_edge = (slab == slabs - 1) & (tile >= grid * (grid - 1))
    left_edge = lax.rem(tile, grid) == 0
    right_edge = lax.rem(tile, grid) == grid - 1
    lane = lax.broadcasted_iota(jnp.int32, (8, LANES), 1)
    first_row = lax.broadcasted_iota(jnp.int32, (8, LANES), 0) == 0
    last_row = lax.broadcasted_iota(jnp.int32, (8, LANES), 0) == 7
    first_lane, last_lane = lane == 0, lane == LANES - 1
    at_left, at_right = left_edge & (lane == first[1]), right_edge & (lane == last[1])

    def across(values, left, right):
        after = [pltpu.roll(p, LANES - 1, 1) for p in values]
        before = [pltpu.roll(p, 1, 1) for p in values]
        out = []
        for j in range(pieces):
            beyond, behind = after[j], before[j]
            if pieces > 1:
                beyond = jnp.where(last_lane, after[(j + 1) % pieces], beyond)
                behind = jnp.where(first_lane, before[(j - 1) % pieces], behind)
            if j == last[0]:
                beyond = jnp.where(at_right, right, beyond)
            if j == first[0]:
                behind = jnp.where(at_left, left, behind)
            out.append(beyond - behind)
        return out

    def slopes(r):
        here = [surface[j, pl.ds(r, 8), :] for j in range(pieces)]
        wide_x = across(here, here[first[0]], here[last[0]])
        at_top = first_row & (top_edge & (r == top))
        at_bottom = last_row & (bottom_edge & (r == bottom - 8))
        wide_y = []
        for j in range(pieces):
            over = jnp.where(at_top, here[j], surface[j, pl.ds(r - 1, 8), :])
            under = jnp.where(at_bottom, here[j], surface[j, pl.ds(r + 1, 8), :])
            wide_y.append(under - over)
        return here, wide_x, wide_y

    zero = jnp.zeros((8, LANES), jnp.float32)

    def bend(r):
        here, wide_x, wide_y = slopes(r)
        inverse = [lax.rsqrt(1.0 + 0.25 * (x * x + y * y)) for x, y in zip(wide_x, wide_y)]
        spread = across([x * w for x, w in zip(wide_x, inverse)], zero, zero)
        level = (top_edge & (r < top)) | (bottom_edge & (r >= bottom))
        for j in range(pieces):
            normal_y[j, pl.ds(r, 8), :] = jnp.where(level, 0.0, wide_y[j] * inverse[j])
            partial[j, pl.ds(r, 8), :] = here[j] + (0.25 * FLOW_STEP) * spread[j]

    def move(r):
        for j in range(pieces):
            surface[j, pl.ds(r, 8), :] = partial[j, pl.ds(r, 8), :] + (0.25 * FLOW_STEP) * (
                normal_y[j, pl.ds(r + 1, 8), :] - normal_y[j, pl.ds(r - 1, 8), :]
            )

    def each(start, count, group, act):
        def step(i, carry):
            for k in range(group):
                act(start + pl.multiple_of((i * group + k) * 8, 8))
            return carry

        lax.fori_loop(0, count // group, step, 0)

    def sweep(i, carry):
        each(8, total // 8 - 2, groups[0], bend)
        each(8, total // 8 - 2, groups[1], move)
        return carry

    if pieces > 1:
        lax.fori_loop(0, SWEEPS, sweep, 0)
        each(0, rows // 8, groups[2], lambda r: finish(r, *slopes(top + r)))
        return

    strips = list(range(8, total - 8, 8))

    def steps(values, above, below):
        up = {r: pltpu.roll(values[r], 7, 0) for r in values}
        down = {r: pltpu.roll(values[r], 1, 0) for r in values}
        out = {}
        for r in strips:
            under = jnp.where(last_row, up.get(r + 8, up[r]), up[r])
            over = jnp.where(first_row, down.get(r - 8, down[r]), down[r])
            if r == bottom - 8:
                under = jnp.where(last_row & bottom_edge, below(values[r]), under)
            if r == top:
                over = jnp.where(first_row & top_edge, above(values[r]), over)
            out[r] = under - over
        return out

    def sweep_block(i, carry):
        values = dict(zip(range(0, total, 8), carry))
        wide_y = steps(values, lambda v: v, lambda v: v)
        upright, moved = {}, {}
        for r in strips:
            (wide_x,) = across([values[r]], values[r], values[r])
            inverse = lax.rsqrt(1.0 + 0.25 * (wide_x * wide_x + wide_y[r] * wide_y[r]))
            upright[r] = wide_y[r] * inverse
            moved[r] = values[r] + (0.25 * FLOW_STEP) * across([wide_x * inverse], zero, zero)[0]
        rise = steps(upright, lambda v: zero, lambda v: zero)
        for r in strips:
            values[r] = moved[r] + (0.25 * FLOW_STEP) * rise[r]
        return tuple(values[r] for r in range(0, total, 8))

    start = tuple(surface[0, r : r + 8, :] for r in range(0, total, 8))
    values = dict(zip(range(0, total, 8), lax.fori_loop(0, SWEEPS, sweep_block, start)))
    wide_y = steps(values, lambda v: v, lambda v: v)
    for r in range(0, rows, 8):
        here = values[top + r]
        finish(r, [here], across([here], here, here), [wide_y[top + r]])


def shaded(wide_x, wide_y, layers, cover):
    x, y = 0.5 * wide_x, 0.5 * wide_y
    inverse = lax.rsqrt(1.0 + (x * x + y * y))
    diffuse = jnp.maximum((0.8 - 0.36 * x - 0.48 * y) * inverse, 0.0)
    gloss = jnp.maximum((0.9487 - 0.1897 * x - 0.253 * y) * inverse, 0.0)
    for _ in range(4):
        gloss = gloss * gloss
    fluid = cover.astype(jnp.float32)
    lit = 0.15 + 0.7 * jnp.exp(-0.8 * functools.reduce(jnp.add, layers)) * diffuse + 0.4 * gloss
    return fluid * lit + (1.0 - fluid) * 0.05


def inner_kernel(rows, grid, above_ref, band_ref, below_ref, thick_ref, cover_ref, smooth_ref, shade_ref, *scratch):
    surface = scratch[0]
    blocks = surface.shape[0]
    for j in range(blocks):
        cols = pl.ds(j * LANES, LANES)
        surface[j, 0:PAD, :] = above_ref[:, cols]
        surface[j, PAD : PAD + rows, :] = band_ref[:, cols]
        surface[j, PAD + rows :, :] = below_ref[:, cols]

    def finish(r, here, wide_x, wide_y):
        span = pl.ds(r, 8)
        for j in range(blocks):
            cols = pl.ds(j * LANES, LANES)
            smooth_ref[span, cols] = here[j]
            shade_ref[span, cols] = shaded(wide_x[j], wide_y[j], [thick_ref[span, cols]], cover_ref[span, cols])

    flow(rows, grid, blocks, (blocks - 1, LANES - 1), (0, 0), (5, 10, 4), *scratch, finish)


def outer_kernel(
    rows,
    grid,
    above_ref,
    band_ref,
    below_ref,
    left_ref,
    right_ref,
    thick_ref,
    cover_ref,
    inner_smooth_ref,
    inner_shade_ref,
    smooth_ref,
    shade_ref,
    *scratch,
):
    surface = scratch[0]
    total = rows + 2 * PAD
    blocks = band_ref.shape[1] // LANES
    quarter = LANES // 4
    lane = lax.broadcasted_iota(jnp.int32, (8, LANES), 1)
    low = lane < LANES // 2

    def own(r, block):
        cols = pl.ds(block * LANES, LANES)
        if r < PAD:
            return above_ref[r : r + 8, cols]
        if r < PAD + rows:
            return band_ref[r - PAD : r - PAD + 8, cols]
        return below_ref[r - PAD - rows : r - PAD - rows + 8, cols]

    size = total // 4
    for r in range(0, total, 8):
        group, row = r // size, r % size
        right = pltpu.roll(right_ref[row : row + 8, :], (5 - group) % 4 * quarter, 1)
        left = pltpu.roll(left_ref[row : row + 8, :], (6 - group) % 4 * quarter, 1)
        at_right = jnp.where(lane < quarter, pltpu.roll(own(r, blocks - 1), quarter, 1), right)
        at_left = jnp.where(lane < 3 * quarter, left, pltpu.roll(own(r, 0), 3 * quarter, 1))
        surface[0, r : r + 8, :] = jnp.where(low, at_right, at_left)
    middle = pl.ds(LANES, (blocks - 2) * LANES)
    smooth_ref[:, middle] = inner_smooth_ref[:, middle]
    shade_ref[:, middle] = inner_shade_ref[:, middle]
    outer = (
        (0, quarter, lane < quarter // 2),
        (blocks - 1, 3 * quarter, lane >= LANES - quarter // 2),
    )

    def finish(r, here, wide_x, wide_y):
        span = pl.ds(r, 8)
        for block, shift, new in outer:
            cols = pl.ds(block * LANES, LANES)
            smooth, x, y = (pltpu.roll(a[0], shift, 1) for a in (here, wide_x, wide_y))
            shade = shaded(x, y, [thick_ref[span, cols]], cover_ref[span, cols])
            smooth_ref[span, cols] = jnp.where(new, smooth, inner_smooth_ref[span, cols])
            shade_ref[span, cols] = jnp.where(new, shade, inner_shade_ref[span, cols])

    flow(rows, grid, 1, (0, quarter - 1), (0, 3 * quarter), (10, 10, 8), *scratch, finish)


def local(depth_layers, thickness_layers, coverage):
    slabs = lax.axis_size("slab")
    grid = math.isqrt(lax.axis_size("tile"))
    slab = lax.axis_index("slab")
    tile = lax.axis_index("tile")
    _, _, height, width = depth_layers.shape
    rows = height // slabs
    core = slab % 2

    parts = lax.all_to_all(
        depth_layers.reshape(slabs, rows, width), "slab", split_axis=0, concat_axis=0, tiled=True
    )
    thick = sum_by_swaps(pair_sum(thickness_layers.reshape(slabs, rows, width)), slab)
    band = jnp.min(parts, axis=0)
    far, near = neighbour_rows(band, grid, slabs, core)
    odd = core == 1
    above, below = jnp.where(odd, near, far), jnp.where(odd, far, near)
    tall = [
        jnp.concatenate([a[:, cut] for a in (above, band, below)], axis=0)
        for cut in (slice(0, LANES), slice(width - LANES, width))
    ]
    left, right = neighbour_columns(*tall, grid, tile % grid)

    vmem = pl.BlockSpec(memory_space=pltpu.VMEM)
    total = rows + 2 * PAD
    blocks = width // LANES
    above, band, below, left, right, thick, cover = (
        pltpu.with_memory_space_constraint(a, pltpu.VMEM)
        for a in (above, band, below, left, right, thick, coverage[0])
    )
    held = pltpu.VMEM((rows, width), jnp.float32)
    inner = pl.pallas_call(
        functools.partial(inner_kernel, rows, grid),
        compiler_params=PARAMS,
        out_shape=(held, held),
        in_specs=[vmem] * 5,
        out_specs=(vmem, vmem),
        scratch_shapes=[pltpu.VMEM((blocks, total, LANES), jnp.float32)] * 3,
    )(above, band, below, thick, cover)
    out = jax.ShapeDtypeStruct((rows, width), jnp.float32)
    smooth, shade = pl.pallas_call(
        functools.partial(outer_kernel, rows, grid),
        compiler_params=PARAMS,
        out_shape=(out, out),
        in_specs=[vmem] * 9,
        out_specs=(vmem, vmem),
        scratch_shapes=[pltpu.VMEM((1, total, LANES), jnp.float32)] * 3,
    )(
        above,
        band,
        below,
        left,
        right,
        thick,
        cover,
        *(pltpu.with_memory_space_constraint(a, pltpu.VMEM) for a in inner),
    )
    return (smooth[None], shade[None])


def solution(mesh):
    return jax.shard_map(
        local,
        mesh=mesh,
        in_specs=(
            P("slab", "tile", None, None),
            P("slab", "tile", None, None),
            P("tile", "slab", None),
        ),
        out_specs=(P("tile", "slab", None), P("tile", "slab", None)),
        check_vma=False,
    )
```

```python
import functools
import math

import jax
import jax.numpy as jnp
from jax import lax
from jax.experimental import pallas as pl
from jax.experimental.pallas import tpu as pltpu
from jax.sharding import PartitionSpec as P

SWEEPS = 4
FLOW_STEP = 0.2

PAD = 16
LANES = 128
PARAMS = pltpu.CompilerParams(vmem_limit_bytes=16 * 1024 * 1024)


def pick_kernel(flip, value_ref, out_ref, sem):
    copy = pltpu.make_async_copy(
        value_ref.at[:, (lax.axis_index("slab") + flip) % 2], out_ref, sem
    )
    copy.start()
    copy.wait()


def pair_sum(value):
    bands, rows, width = value.shape
    value = value.reshape(bands // 2, 2, rows, width)
    value = pltpu.with_memory_space_constraint(value, pltpu.HBM)

    def pick(flip):
        return pl.pallas_call(
            functools.partial(pick_kernel, flip),
            compiler_params=PARAMS,
            out_shape=pltpu.VMEM((bands // 2, rows, width), jnp.float32),
            in_specs=[pl.BlockSpec(memory_space=pltpu.HBM)],
            out_specs=pl.BlockSpec(memory_space=pltpu.VMEM),
            scratch_shapes=[pltpu.SemaphoreType.DMA],
        )(value)

    own = pick(0)
    return own + lax.ppermute(pick(1), "slab", [(i, i ^ 1) for i in range(bands)])


def sum_by_swaps(value, slab):
    slabs = lax.axis_size("slab")
    chips = slabs // 2
    chip = slab // 2

    def share(index):
        return lax.dynamic_index_in_dim(value, index, 0, keepdims=False)

    total = share(chip)
    for step in (3, 2, 1):
        route = [(i, (i // 2 ^ step) * 2 + i % 2) for i in range(slabs)]
        total = total + lax.ppermute(share(chip ^ step), "slab", route)
    return total


def neighbour_rows(band, grid, slabs, core):
    tiles = grid * grid
    across = []
    for t in range(tiles):
        for s in range(1, slabs, 2):
            upper = s * tiles + t
            lower = (s + 1) * tiles + t if s + 1 < slabs else t + grid
            if s + 1 < slabs or t + grid < tiles:
                across += [(upper, lower), (lower, upper)]
    odd = core == 1
    head, tail = band[:PAD], band[-PAD:]
    long = jnp.where(odd, tail, head)
    long = jnp.concatenate([long, long[:, :LANES]], axis=1)
    far = lax.ppermute(long, ("slab", "tile"), across)[:, :-LANES]
    near = lax.ppermute(jnp.where(odd, head, tail), "slab", [(i, i ^ 1) for i in range(slabs)])
    return far, near


def pack(block, start):
    size = block.shape[0] // 4
    return jnp.concatenate(
        [block[k * size : (k + 1) * size, start : start + LANES // 4] for k in range(4)], axis=1
    )


def neighbour_columns(first, last, grid, column):
    odd = column % 2 == 1
    near, far = [], []
    for t in range(grid * grid):
        if t % grid + 1 < grid:
            (near if t % 2 == 0 else far).extend([(t, t + 1), (t + 1, t)])
    first, last = pack(first, 0), pack(last, LANES - LANES // 4)
    long = jnp.where(odd, last, first)
    long = jnp.concatenate([long, long[:8]], axis=0)
    far = lax.ppermute(long, "tile", far)[:-8]
    near = lax.ppermute(jnp.where(odd, first, last), "tile", near)
    return jnp.where(odd, near, far), jnp.where(odd, far, near)


def flow(rows, grid, pieces, last, first, groups, surface, partial, normal_y, finish):
    total = rows + 2 * PAD
    top, bottom = PAD, PAD + rows
    slabs = lax.axis_size("slab")
    slab, tile = lax.axis_index("slab"), lax.axis_index("tile")
    top_edge = (slab == 0) & (tile < grid)
    bottom_edge = (slab == slabs - 1) & (tile >= grid * (grid - 1))
    left_edge = lax.rem(tile, grid) == 0
    right_edge = lax.rem(tile, grid) == grid - 1
    lane = lax.broadcasted_iota(jnp.int32, (8, LANES), 1)
    first_row = lax.broadcasted_iota(jnp.int32, (8, LANES), 0) == 0
    last_row = lax.broadcasted_iota(jnp.int32, (8, LANES), 0) == 7
    first_lane, last_lane = lane == 0, lane == LANES - 1
    at_left, at_right = left_edge & (lane == first[1]), right_edge & (lane == last[1])

    def across(values, left, right):
        after = [pltpu.roll(p, LANES - 1, 1) for p in values]
        before = [pltpu.roll(p, 1, 1) for p in values]
        out = []
        for j in range(pieces):
            beyond, behind = after[j], before[j]
            if pieces > 1:
                beyond = jnp.where(last_lane, after[(j + 1) % pieces], beyond)
                behind = jnp.where(first_lane, before[(j - 1) % pieces], behind)
            if j == last[0]:
                beyond = jnp.where(at_right, right, beyond)
            if j == first[0]:
                behind = jnp.where(at_left, left, behind)
            out.append(beyond - behind)
        return out

    def slopes(r):
        here = [surface[j, pl.ds(r, 8), :] for j in range(pieces)]
        wide_x = across(here, here[first[0]], here[last[0]])
        at_top = first_row & (top_edge & (r == top))
        at_bottom = last_row & (bottom_edge & (r == bottom - 8))
        wide_y = []
        for j in range(pieces):
            over = jnp.where(at_top, here[j], surface[j, pl.ds(r - 1, 8), :])
            under = jnp.where(at_bottom, here[j], surface[j, pl.ds(r + 1, 8), :])
            wide_y.append(under - over)
        return here, wide_x, wide_y

    zero = jnp.zeros((8, LANES), jnp.float32)

    def bend(r):
        here, wide_x, wide_y = slopes(r)
        inverse = [lax.rsqrt(1.0 + 0.25 * (x * x + y * y)) for x, y in zip(wide_x, wide_y)]
        spread = across([x * w for x, w in zip(wide_x, inverse)], zero, zero)
        level = (top_edge & (r < top)) | (bottom_edge & (r >= bottom))
        for j in range(pieces):
            normal_y[j, pl.ds(r, 8), :] = jnp.where(level, 0.0, wide_y[j] * inverse[j])
            partial[j, pl.ds(r, 8), :] = here[j] + (0.25 * FLOW_STEP) * spread[j]

    def move(r):
        for j in range(pieces):
            surface[j, pl.ds(r, 8), :] = partial[j, pl.ds(r, 8), :] + (0.25 * FLOW_STEP) * (
                normal_y[j, pl.ds(r + 1, 8), :] - normal_y[j, pl.ds(r - 1, 8), :]
            )

    def each(start, count, group, act):
        def step(i, carry):
            for k in range(group):
                act(start + pl.multiple_of((i * group + k) * 8, 8))
            return carry

        lax.fori_loop(0, count // group, step, 0)

    def sweep(i, carry):
        each(8, total // 8 - 2, groups[0], bend)
        each(8, total // 8 - 2, groups[1], move)
        return carry

    if pieces > 1:
        lax.fori_loop(0, SWEEPS, sweep, 0)
        each(0, rows // 8, groups[2], lambda r: finish(r, *slopes(top + r)))
        return

    strips = list(range(8, total - 8, 8))

    def steps(values, above, below):
        up = {r: pltpu.roll(values[r], 7, 0) for r in values}
        down = {r: pltpu.roll(values[r], 1, 0) for r in values}
        out = {}
        for r in strips:
            under = jnp.where(last_row, up.get(r + 8, up[r]), up[r])
            over = jnp.where(first_row, down.get(r - 8, down[r]), down[r])
            if r == bottom - 8:
                under = jnp.where(last_row & bottom_edge, below(values[r]), under)
            if r == top:
                over = jnp.where(first_row & top_edge, above(values[r]), over)
            out[r] = under - over
        return out

    def sweep_block(i, carry):
        values = dict(zip(range(0, total, 8), carry))
        wide_y = steps(values, lambda v: v, lambda v: v)
        upright, moved = {}, {}
        for r in strips:
            (wide_x,) = across([values[r]], values[r], values[r])
            inverse = lax.rsqrt(1.0 + 0.25 * (wide_x * wide_x + wide_y[r] * wide_y[r]))
            upright[r] = wide_y[r] * inverse
            moved[r] = values[r] + (0.25 * FLOW_STEP) * across([wide_x * inverse], zero, zero)[0]
        rise = steps(upright, lambda v: zero, lambda v: zero)
        for r in strips:
            values[r] = moved[r] + (0.25 * FLOW_STEP) * rise[r]
        return tuple(values[r] for r in range(0, total, 8))

    start = tuple(surface[0, r : r + 8, :] for r in range(0, total, 8))
    values = dict(zip(range(0, total, 8), lax.fori_loop(0, SWEEPS, sweep_block, start)))
    wide_y = steps(values, lambda v: v, lambda v: v)
    for r in range(0, rows, 8):
        here = values[top + r]
        finish(r, [here], across([here], here, here), [wide_y[top + r]])


def shaded(wide_x, wide_y, layers, cover):
    x, y = 0.5 * wide_x, 0.5 * wide_y
    inverse = lax.rsqrt(1.0 + (x * x + y * y))
    diffuse = jnp.maximum((0.8 - 0.36 * x - 0.48 * y) * inverse, 0.0)
    gloss = jnp.maximum((0.9487 - 0.1897 * x - 0.253 * y) * inverse, 0.0)
    for _ in range(4):
        gloss = gloss * gloss
    fluid = cover.astype(jnp.float32)
    lit = 0.15 + 0.7 * jnp.exp(-0.8 * functools.reduce(jnp.add, layers)) * diffuse + 0.4 * gloss
    return fluid * lit + (1.0 - fluid) * 0.05


def inner_kernel(rows, grid, above_ref, band_ref, below_ref, thick_ref, cover_ref, smooth_ref, shade_ref, *scratch):
    surface = scratch[0]
    blocks = surface.shape[0]
    for j in range(blocks):
        cols = pl.ds(j * LANES, LANES)
        surface[j, 0:PAD, :] = above_ref[:, cols]
        surface[j, PAD : PAD + rows, :] = band_ref[:, cols]
        surface[j, PAD + rows :, :] = below_ref[:, cols]

    def finish(r, here, wide_x, wide_y):
        span = pl.ds(r, 8)
        for j in range(blocks):
            cols = pl.ds(j * LANES, LANES)
            smooth_ref[span, cols] = here[j]
            shade_ref[span, cols] = shaded(wide_x[j], wide_y[j], [thick_ref[span, cols]], cover_ref[span, cols])

    flow(rows, grid, blocks, (blocks - 1, LANES - 1), (0, 0), (5, 10, 4), *scratch, finish)


def outer_kernel(
    rows,
    grid,
    above_ref,
    band_ref,
    below_ref,
    left_ref,
    right_ref,
    thick_ref,
    cover_ref,
    inner_smooth_ref,
    inner_shade_ref,
    smooth_ref,
    shade_ref,
    ends,
    sems,
    *scratch,
):
    surface = scratch[0]
    total = rows + 2 * PAD
    blocks = band_ref.shape[1] // LANES
    quarter = LANES // 4
    lane = lax.broadcasted_iota(jnp.int32, (8, LANES), 1)
    low = lane < LANES // 2

    def own(r, block):
        cols = pl.ds(block * LANES, LANES)
        if r < PAD:
            return above_ref[r : r + 8, cols]
        if r < PAD + rows:
            return band_ref[r - PAD : r - PAD + 8, cols]
        return below_ref[r - PAD - rows : r - PAD - rows + 8, cols]

    size = total // 4
    for r in range(0, total, 8):
        group, row = r // size, r % size
        right = pltpu.roll(right_ref[row : row + 8, :], (5 - group) % 4 * quarter, 1)
        left = pltpu.roll(left_ref[row : row + 8, :], (6 - group) % 4 * quarter, 1)
        at_right = jnp.where(lane < quarter, pltpu.roll(own(r, blocks - 1), quarter, 1), right)
        at_left = jnp.where(lane < 3 * quarter, left, pltpu.roll(own(r, 0), 3 * quarter, 1))
        surface[0, r : r + 8, :] = jnp.where(low, at_right, at_left)
    inner_refs, out_refs = (inner_smooth_ref, inner_shade_ref), (smooth_ref, shade_ref)
    middle = pl.ds(LANES, (blocks - 2) * LANES)
    copies = [
        pltpu.make_async_copy(a.at[:, middle], b.at[:, middle], sems.at[2, k])
        for k, (a, b) in enumerate(zip(inner_refs, out_refs))
    ]
    for copy in copies:
        copy.start()
    outer = (
        (0, quarter, lane < quarter // 2),
        (blocks - 1, 3 * quarter, lane >= LANES - quarter // 2),
    )

    def finish(r, here, wide_x, wide_y):
        span = pl.ds(r, 8)
        for end, (block, shift, new) in enumerate(outer):
            cols = pl.ds(block * LANES, LANES)
            smooth, x, y = (pltpu.roll(a[0], shift, 1) for a in (here, wide_x, wide_y))
            shade = shaded(x, y, [thick_ref[span, cols]], cover_ref[span, cols])
            ends[0, end, span, :] = jnp.where(new, smooth, inner_smooth_ref[span, cols])
            ends[1, end, span, :] = jnp.where(new, shade, inner_shade_ref[span, cols])

    flow(rows, grid, 1, (0, quarter - 1), (0, 3 * quarter), (10, 10, 8), *scratch, finish)
    for k, ref in enumerate(out_refs):
        for end, (block, _, _) in enumerate(outer):
            cols = pl.ds(block * LANES, LANES)
            copy = pltpu.make_async_copy(ends.at[k, end], ref.at[:, cols], sems.at[end, k])
            copy.start()
            copies.append(copy)
    for copy in copies:
        copy.wait()


def local(depth_layers, thickness_layers, coverage):
    slabs = lax.axis_size("slab")
    grid = math.isqrt(lax.axis_size("tile"))
    slab = lax.axis_index("slab")
    tile = lax.axis_index("tile")
    _, _, height, width = depth_layers.shape
    rows = height // slabs
    core = slab % 2

    parts = lax.all_to_all(
        depth_layers.reshape(slabs, rows, width), "slab", split_axis=0, concat_axis=0, tiled=True
    )
    thick = sum_by_swaps(pair_sum(thickness_layers.reshape(slabs, rows, width)), slab)
    band = jnp.min(parts, axis=0)
    far, near = neighbour_rows(band, grid, slabs, core)
    odd = core == 1
    above, below = jnp.where(odd, near, far), jnp.where(odd, far, near)
    tall = [
        jnp.concatenate([a[:, cut] for a in (above, band, below)], axis=0)
        for cut in (slice(0, LANES), slice(width - LANES, width))
    ]
    left, right = neighbour_columns(*tall, grid, tile % grid)

    vmem = pl.BlockSpec(memory_space=pltpu.VMEM)
    total = rows + 2 * PAD
    blocks = width // LANES
    above, band, below, left, right, thick, cover = (
        pltpu.with_memory_space_constraint(a, pltpu.VMEM)
        for a in (above, band, below, left, right, thick, coverage[0])
    )
    held = pltpu.VMEM((rows, width), jnp.float32)
    inner = pl.pallas_call(
        functools.partial(inner_kernel, rows, grid),
        compiler_params=PARAMS,
        out_shape=(held, held),
        in_specs=[vmem] * 5,
        out_specs=(vmem, vmem),
        scratch_shapes=[pltpu.VMEM((blocks, total, LANES), jnp.float32)] * 3,
    )(above, band, below, thick, cover)
    out = jax.ShapeDtypeStruct((rows, width), jnp.float32)
    smooth, shade = pl.pallas_call(
        functools.partial(outer_kernel, rows, grid),
        compiler_params=PARAMS,
        out_shape=(out, out),
        in_specs=[vmem] * 9,
        out_specs=(pl.BlockSpec(memory_space=pltpu.HBM),) * 2,
        scratch_shapes=[
            pltpu.VMEM((2, 2, rows, LANES), jnp.float32),
            pltpu.SemaphoreType.DMA((3, 2)),
            *[pltpu.VMEM((1, total, LANES), jnp.float32)] * 3,
        ],
    )(
        above,
        band,
        below,
        left,
        right,
        thick,
        cover,
        *(pltpu.with_memory_space_constraint(a, pltpu.VMEM) for a in inner),
    )
    return (smooth[None], shade[None])


def solution(mesh):
    return jax.shard_map(
        local,
        mesh=mesh,
        in_specs=(
            P("slab", "tile", None, None),
            P("slab", "tile", None, None),
            P("tile", "slab", None),
        ),
        out_specs=(P("tile", "slab", None), P("tile", "slab", None)),
        check_vma=False,
    )
```
